512 devices in a mesh: zero: 32 (over y, x, core), dp: 16 (over z).
Axes of the slice: x: 4, y: 4, z: 16, core: 2. Of those that a mesh axis runs over, the one named last changes fastest.
Arguments:
- grad_partial: bfloat16 [16, 14, 3584, 256], P('dp', None, 'zero'), may hold values from -150 to 150
- momentum: float32 [14, 3584, 256], P(None, 'zero'), may hold values from -150 to 150
- shapes: int32 [14, 2], replicated, may hold values from 128 to 3584, as said below
- owners: int32 [14], replicated, may hold values from 0 to 31, as said below
Outputs:
- new_momentum: float32 [14, 3584, 256], P(None, 'zero')
- update: bfloat16 [14, 3584, 256], P(None, 'zero')
- owner_norms: float32 [32, 1], P('zero')
The draws below stay inside these ranges and needn't reach their ends.
Inputs may be any that keep to these rules, and one draw needn't show every extreme that they name: `shapes`: column 0 is a multiple of 16 from 1792 to 3584, column 1 a multiple of 8 from 128 to 256; some matrix is live in full. `owners`: each owner holds at most 1 matrix, and some owner holds 1.
All inputs are finite; a program needn't handle non-finite values.
Results may differ from the reference program's by a relative error of at most 0.03.
Values may be sent and summed in bfloat16 or wider, within the bound.
A program may use at most 64 MiB of HBM per device.

```python
import math
import jax
import jax.numpy as jnp
from jax import lax

LONG = 3584
SHORT = 256
MATS = 14
ITERS = 3
MOST = 1
N_ZERO = 32
N_DP = 16


def shared_scales(key):
    first, second = jax.random.split(key)
    row_scale = jnp.exp(jax.random.uniform(first, (MATS, LONG), minval=math.log(0.3), maxval=math.log(3.0)))
    ramp = jnp.exp(math.log(3.0) * jnp.arange(LONG, dtype=jnp.float32) / LONG)
    col_scale = jnp.exp(jax.random.uniform(second, (MATS, SHORT), minval=math.log(0.3), maxval=math.log(3.0)))
    return (row_scale * ramp[None, :], col_scale)


def draw_grad_partial(key, part):
    row_scale, col_scale = shared_scales(key)
    key = jax.random.fold_in(key, 11)
    raw = jnp.clip(jax.random.normal(key, (N_DP, MATS, LONG, SHORT)), -5.0, 5.0) / math.sqrt(N_DP)
    return (raw * row_scale[None, :, :, None] * col_scale[None, :, None, :]).astype(jnp.bfloat16)


def draw_momentum(key, part):
    row_scale, col_scale = shared_scales(key)
    key = jax.random.fold_in(key, 12)
    raw = jnp.clip(jax.random.normal(key, (MATS, LONG, SHORT)), -5.0, 5.0)
    return (raw * row_scale[:, :, None] * col_scale[:, None, :]).astype(jnp.float32)


def draw_shapes(key, part):
    key = jax.random.fold_in(key, 13)
    first, second, third = jax.random.split(key, 3)
    live_rows = LONG - 16 * jax.random.randint(first, (MATS,), 0, LONG // 32 + 1)
    live_cols = SHORT - 8 * jax.random.randint(second, (MATS,), 0, SHORT // 16 + 1)
    full_index = jax.random.randint(third, (), 0, MATS)
    index_ids = jnp.arange(MATS)
    live_rows = jnp.where(index_ids == full_index, LONG, live_rows)
    live_cols = jnp.where(index_ids == full_index, SHORT, live_cols)
    return jnp.stack([live_rows, live_cols], axis=1).astype(jnp.int32)


def draw_owners(key, part):
    key = jax.random.fold_in(key, 14)
    first, second = jax.random.split(key)
    devices = jax.random.permutation(first, N_ZERO)
    order = jax.random.permutation(second, MATS)
    index_ids = jnp.arange(MATS)
    pattern = index_ids % N_ZERO
    return jnp.zeros((MATS,), jnp.int32).at[order].set(devices[pattern].astype(jnp.int32))


def setup_inputs(seed: int = 0) -> dict:
    key_of = jax.random.split(jax.random.key(seed), 5)
    grad_partial = draw_grad_partial(jax.random.fold_in(key_of[4], 71), 0)
    momentum = draw_momentum(jax.random.fold_in(key_of[4], 71), 0)
    shapes = draw_shapes(jax.random.fold_in(key_of[4], 71), 0)
    owners = draw_owners(jax.random.fold_in(key_of[4], 71), 0)
    return {"grad_partial": grad_partial, "momentum": momentum, "shapes": shapes, "owners": owners}


coef_a = 3.4445
coef_b = -4.775
coef_c = 2.0315
epsilon = 1e-07
momentum_decay = 0.95

def orthogonal(nesterov_one):
    wide = nesterov_one.astype(jnp.float32)
    norm_value = jnp.sqrt(jnp.sum(wide * wide))
    state = (wide / (norm_value + epsilon)).astype(jnp.bfloat16)
    for sweep in range(ITERS):
        gram = jnp.dot(state.T, state, preferred_element_type=jnp.float32).astype(jnp.bfloat16)
        square = jnp.dot(gram, gram, preferred_element_type=jnp.float32)
        poly = (coef_b * gram.astype(jnp.float32) + coef_c * square).astype(jnp.bfloat16)
        state = (coef_a * state.astype(jnp.float32) + jnp.dot(state, poly, preferred_element_type=jnp.float32)).astype(jnp.bfloat16)
    return (state, norm_value)

def reference(grad_partial, momentum, shapes, owners):
    row_ids = jnp.arange(LONG, dtype=jnp.int32)[None, :, None]
    col_ids = jnp.arange(SHORT, dtype=jnp.int32)[None, None, :]
    live_mask = (row_ids < shapes[:, 0][:, None, None]) & (col_ids < shapes[:, 1][:, None, None])
    gradient = jnp.where(live_mask, lax.optimization_barrier(jnp.sum(grad_partial, axis=0, dtype=jnp.float32)), jnp.float32(0.0))
    new_momentum = jnp.where(live_mask, momentum_decay * momentum + gradient, jnp.float32(0.0))
    nesterov = (gradient + momentum_decay * new_momentum).astype(jnp.bfloat16)
    finals, norms = lax.map(orthogonal, nesterov)
    scale_factor = 0.2 * jnp.sqrt(jnp.maximum(shapes[:, 0], shapes[:, 1]).astype(jnp.float32))
    update = (finals.astype(jnp.float32) * scale_factor[:, None, None]).astype(jnp.bfloat16)
    live_area = (shapes[:, 0] * shapes[:, 1]).astype(jnp.float32)
    root_mean = norms / jnp.sqrt(live_area)
    index_ids = jnp.arange(MATS, dtype=jnp.int32)
    slot_rank = lax.optimization_barrier(jnp.sum((owners[:, None] == owners[None, :]) & (index_ids[None, :] < index_ids[:, None]), axis=1)).astype(jnp.int32)
    owner_ids = jnp.arange(N_ZERO, dtype=jnp.int32)[:, None, None]
    rank_ids = jnp.arange(MOST, dtype=jnp.int32)[None, :, None]
    picked = (owners[None, None, :] == owner_ids) & (slot_rank[None, None, :] == rank_ids)
    owner_norms = lax.optimization_barrier(jnp.sum(jnp.where(picked, root_mean[None, None, :], jnp.float32(0.0)), axis=2))
    return (new_momentum, update, owner_norms)
```

```python
import functools

import jax
import jax.numpy as jnp
from jax import lax
from jax.experimental import pallas as pl
from jax.experimental.pallas import tpu as pltpu
from jax.sharding import PartitionSpec as P

ITERS = 3
coef_a = 3.4445
coef_b = -4.775
coef_c = 2.0315
epsilon = 1e-07
momentum_decay = 0.95

MESH = pl.DeviceIdType.MESH
F32, BF16 = jnp.float32, jnp.bfloat16

PARENT = {8: 6, 7: 6, 6: 4, 5: 4, 4: 2, 3: 2, 2: 0, 1: 0}
REDUCE_ORDER = (8, 7, 5, 6, 3, 4, 1, 2)
SIDES = (1, -1)
PARTS = ((0, 64, (8, 7)), (64, 48, (7, 8)))
EXTRA = 16


def children(node, reach):
    return [c for c in sorted(PARENT, reverse=True) if PARENT[c] == node and c <= reach]


def split(value):
    high = value.astype(BF16)
    return high, (value - high.astype(F32)).astype(BF16)


def dot(a, b):
    return jnp.dot(a, b, preferred_element_type=F32)


def kernel(
    mats, n_dp, n_zero, shapes_ref, owners_ref, grad_ref, mom_ref, sum_ref, upd_ref, norm_ref,
    grads, moms, sums, upds, arrived_a, arrived_b, outgoing_a, outgoing_b, nest, gram, slabs, whole,
    load_sem, store_sem, rs_send, rs_recv, ag_send, ag_recv, plane_send, plane_recv,
):
    layer = lax.axis_index("dp")
    me = lax.axis_index("zero")
    shard, short = grads.shape[1:]
    slab = short // n_zero
    arrived, outgoing = (arrived_a, arrived_b), (outgoing_a, outgoing_b)
    owner = layer < mats
    mine = jnp.minimum(layer, mats - 1)

    load_grads = pltpu.make_async_copy(grad_ref.at[0], grads, load_sem.at[0])
    load_grads.start()
    load_moms = pltpu.make_async_copy(mom_ref.at[mine], moms, load_sem.at[1])
    load_moms.start()

    def along(step):
        return lax.rem(layer + (step + n_dp), n_dp)

    barrier = pltpu.get_barrier_semaphore()
    hops = sorted({c - p for c, p in PARENT.items()})
    for hop in hops:
        for side in SIDES:
            pl.semaphore_signal(barrier, inc=1, device_id={"dp": along(side * hop)}, device_id_type=MESH)

    def greet(step, carry):
        pl.semaphore_signal(barrier, inc=1, device_id={"zero": lax.rem(me + step, n_zero)}, device_id_type=MESH)
        return carry

    lax.fori_loop(1, n_zero, greet, 0)
    load_grads.wait()
    load_moms.wait()
    pl.semaphore_wait(barrier, 2 * len(hops) + n_zero - 1)

    def reduce_copy(part, s, node, source):
        return pltpu.make_async_remote_copy(
            src_ref=source,
            dst_ref=arrived[part].at[s, node],
            send_sem=rs_send.at[part, s, node],
            recv_sem=rs_recv.at[part, s, node],
            device_id={"dp": along(SIDES[s] * (node - PARENT[node]))},
            device_id_type=MESH,
        )

    def own_rows(part, j):
        first, rows, _ = PARTS[part]
        return grads.at[j, pl.ds(first, rows)]

    def collected(part, s, node, total):
        for child in children(node, PARTS[part][2][s]):
            reduce_copy(part, s, child, arrived[part].at[s, child]).wait_recv()
            total = total + arrived[part][s, child].astype(F32)
        return total

    def reduce_source(part, s, node, j):
        if children(node, PARTS[part][2][s]):
            return outgoing[part].at[s, node]
        return own_rows(part, j)

    for node in REDUCE_ORDER:
        for s, side in enumerate(SIDES):
            j = along(side * node)

            @pl.when(j < mats)
            def _():
                for part in range(len(PARTS)):
                    if node > PARTS[part][2][s]:
                        continue
                    if children(node, PARTS[part][2][s]):
                        total = collected(part, s, node, own_rows(part, j)[...].astype(F32))
                        outgoing[part][s, node] = total.astype(BF16)
                    reduce_copy(part, s, node, reduce_source(part, s, node, j)).start()

    def spread_copy(which, buffer, part, s, node, j):
        first, rows, _ = PARTS[part]
        if which == 1 and part == len(PARTS) - 1:
            rows += EXTRA
        window = buffer.at[j, pl.ds(first, rows)]
        return pltpu.make_async_remote_copy(
            src_ref=window,
            dst_ref=window,
            send_sem=ag_send.at[which, part, s, node],
            recv_sem=ag_recv.at[which, part, s, node],
            device_id={"dp": along(SIDES[s] * (node - PARENT[node]))},
            device_id_type=MESH,
        )

    def spread_from(which, buffer, part, s, node, j):
        for child in children(node, PARTS[part][2][s]):
            spread_copy(which, buffer, part, s, child, j).start()

    def spread_start(which, buffer):
        for part in range(len(PARTS)):
            for s in range(2):
                spread_from(which, buffer, part, s, 0, layer)

    def spread_forward(which, buffer, nodes):
        for node in nodes:
            for s, side in enumerate(SIDES):
                j = along(-side * node)

                @pl.when(j < mats)
                def _():
                    for part in range(len(PARTS)):
                        if node > PARTS[part][2][s]:
                            continue
                        spread_copy(which, buffer, part, s, node, j).wait_recv()
                        spread_from(which, buffer, part, s, node, j)

    def spread_sent(which, buffer):
        for node in PARENT:
            for s, side in enumerate(SIDES):
                j = along(-side * PARENT[node])

                @pl.when(j < mats)
                def _():
                    for part in range(len(PARTS)):
                        if node <= PARTS[part][2][s]:
                            spread_copy(which, buffer, part, s, node, j).wait_send()

    def plane_copy(source, target, which, peer):
        return pltpu.make_async_remote_copy(
            src_ref=source,
            dst_ref=target,
            send_sem=plane_send.at[which],
            recv_sem=plane_recv.at[which],
            device_id={"zero": peer},
            device_id_type=MESH,
        )

    def slab_of(ref, index):
        return ref.at[pl.ds(pl.multiple_of(index * slab, slab), slab)]

    def plane_wait(which):
        view = whole.at[pl.ds(0, short - slab)]
        return plane_copy(view, view, which, lax.rem(me + 1, n_zero))

    @pl.when(owner)
    def _():
        row_ids = me * shard + lax.broadcasted_iota(jnp.int32, (shard, short), 0)
        col_ids = lax.broadcasted_iota(jnp.int32, (shard, short), 1)
        live = (row_ids < shapes_ref[mine, 0]) & (col_ids < shapes_ref[mine, 1])
        totals = []
        for part in range(len(PARTS)):
            total = own_rows(part, layer)[...].astype(F32)
            for s in range(2):
                total = collected(part, s, 0, total)
            totals.append(total)
        gradient = jnp.where(live, jnp.concatenate(totals, axis=0), 0.0)
        sums[layer] = gradient.astype(BF16)
        spread_start(0, sums)
        new_momentum = jnp.where(live, momentum_decay * moms[...] + gradient, 0.0)
        nesterov = (gradient + momentum_decay * new_momentum).astype(BF16)
        nest[0:shard] = nesterov
        nest[shard:] = jnp.zeros((nest.shape[0] - shard, short), BF16)
        tall = nest[...]
        gram[...] = lax.dot_general(tall, tall, (((0,), (0,)), ((), ())), preferred_element_type=F32)

        def send(step, carry):
            peer = lax.rem(me + step, n_zero)
            plane_copy(slab_of(gram, peer), slabs.at[me], 0, peer).start()
            return carry

        lax.fori_loop(1, n_zero, send, 0)
        slabs[me] = slab_of(gram, me)[...]

    spread_forward(0, sums, (2, 1))

    @pl.when(owner)
    def _():
        plane_wait(0).wait_recv()
        total = jnp.sum(slabs[...], axis=0)
        slab_of(whole, me)[...] = total

        def send(step, carry):
            plane_copy(slab_of(whole, me), slab_of(whole, me), 1, lax.rem(me + step, n_zero)).start()
            return carry

        lax.fori_loop(1, n_zero, send, 0)

    spread_forward(0, sums, (4, 3, 6, 5))

    @pl.when(owner)
    def _():
        plane_wait(1).wait_recv()
        full = whole[...]
        on_diagonal = lax.broadcasted_iota(jnp.int32, (short, short), 0) == lax.broadcasted_iota(
            jnp.int32, (short, short), 1
        )
        square = jnp.where(on_diagonal, full, 0.0)
        square = jnp.sum(jnp.sum(square, axis=0, keepdims=True), axis=1, keepdims=True)
        norm = jnp.sqrt(square)
        inverse = 1.0 / (norm + epsilon)
        a = full * (inverse * inverse)
        state = (nest[...].astype(F32) * inverse).astype(BF16)
        for sweep in range(ITERS):
            a_high, a_low = split(a)
            poly = (coef_b * a_high.astype(F32) + coef_c * dot(a_high, a_high)).astype(BF16)
            if sweep < ITERS - 1:
                half = coef_a * a + dot(a_high, poly) + dot(a_low, poly)
                half_high, half_low = split(half)
                a = coef_a * half + dot(poly, half_high) + dot(poly, half_low)
            state = (coef_a * state.astype(F32) + dot(state, poly)).astype(BF16)
        longest = jnp.maximum(shapes_ref[mine, 0], shapes_ref[mine, 1]).astype(F32)
        scale = 0.2 * jnp.sqrt(jnp.full((1, 1), longest, F32))
        upds[layer, 0:shard] = (state[0:shard].astype(F32) * scale).astype(BF16)
        one = jnp.broadcast_to(norm, (EXTRA, short))
        high, rest = split(one)
        low, rest = split(one - high.astype(F32))
        place = lax.broadcasted_iota(jnp.int32, (EXTRA, short), 0)
        upds[layer, shard:] = jnp.where(
            place == 0, high.astype(F32), jnp.where(place == 1, low.astype(F32), jnp.where(place == 2, rest.astype(F32), 0.0))
        ).astype(BF16)
        spread_start(1, upds)

    spread_forward(0, sums, (8, 7))
    store_sums = pltpu.make_async_copy(sums, sum_ref, store_sem.at[0])
    store_sums.start()

    spread_forward(1, upds, (2, 1, 4, 3, 6, 5, 8, 7))
    store_upds = pltpu.make_async_copy(upds.at[:, pl.ds(0, shard)], upd_ref, store_sem.at[1])
    store_upds.start()

    result = jnp.zeros((1, short), F32)
    for k in range(mats):
        area = (shapes_ref[k, 0] * shapes_ref[k, 1]).astype(F32)
        norm = jnp.sum(upds[k, shard:].astype(F32), axis=0, keepdims=True)
        held = jnp.full((1, short), owners_ref[k], jnp.int32) == me
        result = result + jnp.where(held, norm / jnp.sqrt(jnp.full((1, short), area, F32)), 0.0)
    norm_ref[...] = jnp.broadcast_to(result[:, 0:128], (8, 128))

    for node in PARENT:
        for s, side in enumerate(SIDES):
            j = along(side * node)

            @pl.when(j < mats)
            def _():
                for part in range(len(PARTS)):
                    if node <= PARTS[part][2][s]:
                        reduce_copy(part, s, node, reduce_source(part, s, node, j)).wait_send()

    spread_sent(0, sums)
    spread_sent(1, upds)

    @pl.when(owner)
    def _():
        plane_wait(0).wait_send()
        plane_wait(1).wait_send()

    store_sums.wait()
    store_upds.wait()


def per_device(n_dp, n_zero, grad_partial, momentum, shapes, owners):
    mats, shard, short = momentum.shape
    smem = pl.BlockSpec(memory_space=pltpu.SMEM)
    anywhere = pl.BlockSpec(memory_space=pl.ANY)
    slots = 9
    sums, update, norms = pl.pallas_call(
        functools.partial(kernel, mats, n_dp, n_zero),
        out_shape=(
            jax.ShapeDtypeStruct((mats, shard, short), BF16),
            jax.ShapeDtypeStruct((mats, shard, short), BF16),
            jax.ShapeDtypeStruct((8, 128), F32),
        ),
        in_specs=[smem, smem, anywhere, anywhere],
        out_specs=(anywhere, anywhere, pl.BlockSpec(memory_space=pltpu.VMEM)),
        scratch_shapes=[
            pltpu.VMEM((mats, shard, short), BF16),
            pltpu.VMEM((shard, short), F32),
            pltpu.VMEM((mats, shard, short), BF16),
            pltpu.VMEM((mats, shard + EXTRA, short), BF16),
            pltpu.VMEM((2, slots, PARTS[0][1], short), BF16),
            pltpu.VMEM((2, slots, PARTS[1][1], short), BF16),
            pltpu.VMEM((2, slots, PARTS[0][1], short), BF16),
            pltpu.VMEM((2, slots, PARTS[1][1], short), BF16),
            pltpu.VMEM((128, short), BF16),
            pltpu.VMEM((short, short), F32),
            pltpu.VMEM((n_zero, short // n_zero, short), F32),
            pltpu.VMEM((short, short), F32),
            pltpu.SemaphoreType.DMA((2,)),
            pltpu.SemaphoreType.DMA((2,)),
            pltpu.SemaphoreType.DMA((len(PARTS), 2, slots)),
            pltpu.SemaphoreType.DMA((len(PARTS), 2, slots)),
            pltpu.SemaphoreType.DMA((2, len(PARTS), 2, slots)),
            pltpu.SemaphoreType.DMA((2, len(PARTS), 2, slots)),
            pltpu.SemaphoreType.DMA((2,)),
            pltpu.SemaphoreType.DMA((2,)),
        ],
        compiler_params=pltpu.CompilerParams(
            collective_id=0, has_side_effects=True, vmem_limit_bytes=32 * 1024 * 1024
        ),
    )(shapes, owners, grad_partial, momentum)
    row_ids = lax.axis_index("zero") * shard + lax.broadcasted_iota(jnp.int32, (1, shard, 1), 1)
    col_ids = lax.broadcasted_iota(jnp.int32, (1, 1, short), 2)
    live = (row_ids < shapes[:, 0][:, None, None]) & (col_ids < shapes[:, 1][:, None, None])
    new_momentum = jnp.where(live, momentum_decay * momentum + sums.astype(F32), 0.0)
    return new_momentum, update, norms[0:1, 0:1]


def solution(mesh):
    in_specs = (P("dp", None, "zero", None), P(None, "zero", None), P(), P())
    out_specs = (P(None, "zero", None), P(None, "zero", None), P("zero", None))
    return jax.shard_map(
        functools.partial(per_device, mesh.shape["dp"], mesh.shape["zero"]),
        mesh=mesh, in_specs=in_specs, out_specs=out_specs, check_vma=False,
    )
```

```python
import functools

import jax
import jax.numpy as jnp
from jax import lax
from jax.experimental import pallas as pl
from jax.experimental.pallas import tpu as pltpu
from jax.sharding import PartitionSpec as P

ITERS = 3
coef_a = 3.4445
coef_b = -4.775
coef_c = 2.0315
epsilon = 1e-07
momentum_decay = 0.95

MESH = pl.DeviceIdType.MESH
F32, BF16 = jnp.float32, jnp.bfloat16

PARENT = {8: 6, 7: 6, 6: 4, 5: 4, 4: 2, 3: 2, 2: 0, 1: 0}
SIDES = (1, -1)
PARTS = ((0, 64, (8, 7)), (64, 48, (7, 8)))
SIDE_X, SIDE_Y = 4, 4
EXTRA = 16


def children(node, reach):
    return [c for c in sorted(PARENT, reverse=True) if PARENT[c] == node and c <= reach]


def split(value):
    high = value.astype(BF16)
    return high, (value - high.astype(F32)).astype(BF16)


def dot(a, b):
    return jnp.dot(a, b, preferred_element_type=F32)


def plane_moves():
    def far(step, size):
        return min(step, size - step)

    moves = [(y, x, c) for y in range(SIDE_Y) for x in range(SIDE_X) for c in range(2)][1:]
    return sorted(moves, key=lambda m: -(far(m[0], SIDE_Y) + far(m[1], SIDE_X)))


def kernel(
    mats, n_dp, n_zero, shapes_ref, grad_ref, mom_ref, new_ref, upd_ref,
    grads, moms, sums, news, own, arrived_a, arrived_b, outgoing_a, outgoing_b, nest, gram, slabs, whole,
    load_sem, store_sem, met_sem, rs_send, rs_recv, ag_send, ag_recv, plane_send, plane_recv,
):
    layer = lax.axis_index("dp")
    me = lax.axis_index("zero")
    shard, short = grads.shape[1:]
    slab = short // n_zero
    arrived, outgoing = (arrived_a, arrived_b), (outgoing_a, outgoing_b)
    owner = layer < mats
    mine = jnp.minimum(layer, mats - 1)

    load_grads = pltpu.make_async_copy(grad_ref.at[0], grads, load_sem.at[0])
    load_grads.start()
    load_moms = pltpu.make_async_copy(mom_ref, moms, load_sem.at[1])
    load_moms.start()

    def along(step):
        return lax.rem(layer + (step + n_dp), n_dp)

    core, here_x, here_y = lax.rem(me, 2), lax.rem(me // 2, SIDE_X), me // (2 * SIDE_X)

    def beside(move):
        y, x, c = move
        there_y = lax.rem(here_y + (y + SIDE_Y), SIDE_Y)
        there_x = lax.rem(here_x + (x + SIDE_X), SIDE_X)
        return (there_y * SIDE_X + there_x) * 2 + lax.rem(core + c, 2)

    def greet(semaphore, where):
        pl.semaphore_signal(semaphore, inc=1, device_id=where, device_id_type=MESH)

    barrier = pltpu.get_barrier_semaphore()
    hops = sorted({c - p for c, p in PARENT.items()})
    for hop in hops:
        for side in SIDES:
            greet(barrier, {"dp": along(side * hop)})
    rows_x, rows_y, pair = ((0, 1, 0), (0, -1, 0)), ((1, 0, 0), (-1, 0, 0)), ((0, 0, 1),)
    for move in rows_x + rows_y + pair:
        greet(barrier, {"zero": beside(move)})
    load_grads.wait()
    pl.semaphore_wait(barrier, 2 * len(hops) + 5)
    rounds = (rows_x, pair, rows_y, ((1, 0, 0),))

    def meet(index):
        if index > 0:
            pl.semaphore_wait(met_sem.at[index - 1], len(rounds[index - 1]))
        if index < len(rounds):
            for move in rounds[index]:
                greet(met_sem.at[index], {"zero": beside(move)})

    meet(0)

    def reduce_copy(part, s, node, source):
        return pltpu.make_async_remote_copy(
            src_ref=source,
            dst_ref=arrived[part].at[s, node],
            send_sem=rs_send.at[part, s, node],
            recv_sem=rs_recv.at[part, s, node],
            device_id={"dp": along(SIDES[s] * (node - PARENT[node]))},
            device_id_type=MESH,
        )

    def own_rows(part, j):
        first, rows, _ = PARTS[part]
        return grads.at[j, pl.ds(first, rows)]

    def collected(part, s, node, total):
        for child in children(node, PARTS[part][2][s]):
            reduce_copy(part, s, child, arrived[part].at[s, child]).wait_recv()
            total = total + arrived[part][s, child].astype(F32)
        return total

    def reduce_source(part, s, node, j):
        if children(node, PARTS[part][2][s]):
            return outgoing[part].at[s, node]
        return own_rows(part, j)

    def reduce_step(node):
        for s, side in enumerate(SIDES):
            j = along(side * node)

            @pl.when(j < mats)
            def _():
                for part in range(len(PARTS)):
                    if node > PARTS[part][2][s]:
                        continue
                    if children(node, PARTS[part][2][s]):
                        total = collected(part, s, node, own_rows(part, j)[...].astype(F32))
                        outgoing[part][s, node] = total.astype(BF16)
                    reduce_copy(part, s, node, reduce_source(part, s, node, j)).start()

    for node in (8, 7, 5, 6):
        reduce_step(node)
    meet(1)
    for node in (3, 4):
        reduce_step(node)
    meet(2)
    for node in (1, 2):
        reduce_step(node)
    meet(3)

    def spread_copy(which, part, s, node, j):
        first, rows, _ = PARTS[part]
        if which == 1 and part == len(PARTS) - 1:
            rows += EXTRA
        window = (sums, upd_ref)[which].at[j, pl.ds(first, rows)]
        source = window
        if which == 1 and PARENT[node] == 0:
            source = own.at[pl.ds(first, rows)]
        return pltpu.make_async_remote_copy(
            src_ref=source,
            dst_ref=window,
            send_sem=ag_send.at[which, part, s, node],
            recv_sem=ag_recv.at[which, part, s, node],
            device_id={"dp": along(SIDES[s] * (node - PARENT[node]))},
            device_id_type=MESH,
        )

    def spread_step(which, node):
        for s, side in enumerate(SIDES):
            if node == 0 and s == 1:
                continue
            j = along(-side * node)

            @pl.when(j < mats)
            def _():
                sides = (0, 1) if node == 0 else (s,)
                last = []
                for part in range(len(PARTS)):
                    for t in sides:
                        reach = PARTS[part][2][t]
                        if node > reach:
                            continue
                        if node > 0:
                            spread_copy(which, part, t, node, j).wait_recv()
                        for child in children(node, reach):
                            copy = spread_copy(which, part, t, child, j)
                            if children(child, reach):
                                copy.start()
                            else:
                                last.append(copy)
                for copy in last:
                    copy.start()

    def spread_sent(which):
        for node in PARENT:
            for s, side in enumerate(SIDES):
                j = along(-side * PARENT[node])

                @pl.when(j < mats)
                def _():
                    for part in range(len(PARTS)):
                        if node <= PARTS[part][2][s]:
                            spread_copy(which, part, s, node, j).wait_send()

    def plane_copy(source, target, which, peer):
        return pltpu.make_async_remote_copy(
            src_ref=source,
            dst_ref=target,
            send_sem=plane_send.at[which],
            recv_sem=plane_recv.at[which],
            device_id={"zero": peer},
            device_id_type=MESH,
        )

    def slab_of(ref, index):
        return ref.at[pl.ds(pl.multiple_of(index * slab, slab), slab)]

    def plane_wait(which):
        view = whole.at[pl.ds(0, short - slab)]
        return plane_copy(view, view, which, lax.rem(me + 1, n_zero))

    row_ids = me * shard + lax.broadcasted_iota(jnp.int32, (shard, short), 0)
    col_ids = lax.broadcasted_iota(jnp.int32, (shard, short), 1)

    def live_part(j):
        return (row_ids < shapes_ref[0, j]) & (col_ids < shapes_ref[1, j])

    def new_momentum(j, gradient):
        news[j] = jnp.where(live_part(j), momentum_decay * moms[j] + gradient, 0.0)

    load_moms.wait()
    meet(4)

    @pl.when(owner)
    def _():
        totals = []
        for part in range(len(PARTS)):
            total = own_rows(part, layer)[...].astype(F32)
            for s in range(2):
                total = collected(part, s, 0, total)
            totals.append(total)
        live = live_part(mine)
        gradient = jnp.where(live, jnp.concatenate(totals, axis=0), 0.0)
        sums[layer] = gradient.astype(BF16)
        momentum = jnp.where(live, momentum_decay * moms[layer] + gradient, 0.0)
        nesterov = (gradient + momentum_decay * momentum).astype(BF16)
        nest[0:shard] = nesterov
        nest[shard:] = jnp.zeros((nest.shape[0] - shard, short), BF16)
        tall = nest[...]
        gram[...] = lax.dot_general(tall, tall, (((0,), (0,)), ((), ())), preferred_element_type=F32)
        for move in plane_moves():
            peer = beside(move)
            plane_copy(slab_of(gram, peer), slabs.at[me], 0, peer).start()
        slabs[me] = slab_of(gram, me)[...]

    spread_step(0, 0)
    spread_step(0, 2)

    @pl.when(owner)
    def _():
        plane_wait(0).wait_recv()
        slab_of(whole, me)[...] = jnp.sum(slabs[...], axis=0)
        for move in plane_moves():
            plane_copy(slab_of(whole, me), slab_of(whole, me), 1, beside(move)).start()

    spread_step(0, 4)

    @pl.when(owner)
    def _():
        plane_wait(1).wait_recv()
        full = whole[...]
        on_diagonal = lax.broadcasted_iota(jnp.int32, (short, short), 0) == lax.broadcasted_iota(
            jnp.int32, (short, short), 1
        )
        square = jnp.where(on_diagonal, full, 0.0)
        square = jnp.sum(jnp.sum(square, axis=0, keepdims=True), axis=1, keepdims=True)
        norm = jnp.sqrt(square)
        inverse = 1.0 / (norm + epsilon)
        a = full * (inverse * inverse)
        state = (nest[...].astype(F32) * inverse).astype(BF16)
        for sweep in range(ITERS):
            a_high, a_low = split(a)
            poly = (coef_b * a_high.astype(F32) + coef_c * dot(a_high, a_high)).astype(BF16)
            if sweep < ITERS - 1:
                half = coef_a * a + dot(a_high, poly) + dot(a_low, poly)
                half_high, half_low = split(half)
                a = coef_a * half + dot(poly, half_high) + dot(poly, half_low)
            state = (coef_a * state.astype(F32) + dot(state, poly)).astype(BF16)
        longest = jnp.maximum(shapes_ref[0, mine], shapes_ref[1, mine]).astype(F32)
        scale = 0.2 * jnp.sqrt(jnp.full((1, 1), longest, F32))
        own[0:shard] = (state[0:shard].astype(F32) * scale).astype(BF16)
        one = jnp.broadcast_to(norm, (EXTRA, short))
        high, rest = split(one)
        low, rest = split(one - high.astype(F32))
        place = lax.broadcasted_iota(jnp.int32, (EXTRA, short), 0)
        own[shard:] = jnp.where(
            place == 0, high.astype(F32), jnp.where(place == 1, low.astype(F32), jnp.where(place == 2, rest.astype(F32), 0.0))
        ).astype(BF16)

    spread_step(1, 0)
    keep = pltpu.make_async_copy(own, upd_ref.at[mine], store_sem.at[0])

    @pl.when(owner)
    def _():
        keep.start()

    def new_momenta(node):
        if node == 8:
            j = along(8)

            @pl.when(j < mats)
            def _():
                new_momentum(j, sums[j].astype(F32))
            return
        for s, side in enumerate(SIDES):
            if node == 0 and s == 1:
                continue
            j = along(-side * node)

            @pl.when(j < mats)
            def _():
                new_momentum(j, sums[j].astype(F32))

    spread_step(0, 6)
    spread_step(0, 1)
    for node in (0, 1, 2):
        new_momenta(node)
    spread_step(1, 2)
    spread_step(0, 3)
    for node in (3, 4):
        new_momenta(node)
    spread_step(1, 4)
    spread_step(0, 5)
    for node in (5, 6):
        new_momenta(node)
    spread_step(1, 6)
    for node in (7, 8):
        spread_step(0, node)
        new_momenta(node)
    store_news = pltpu.make_async_copy(news, new_ref, store_sem.at[1])
    store_news.start()

    for node in PARENT:
        for s, side in enumerate(SIDES):
            j = along(side * node)

            @pl.when(j < mats)
            def _():
                for part in range(len(PARTS)):
                    if node <= PARTS[part][2][s]:
                        reduce_copy(part, s, node, reduce_source(part, s, node, j)).wait_send()

    spread_sent(0)

    @pl.when(owner)
    def _():
        plane_wait(0).wait_send()
        plane_wait(1).wait_send()
        keep.wait()

    for node in (1, 3, 5, 7, 8):
        spread_step(1, node)
    spread_sent(1)
    store_news.wait()


def finish(mats, shapes_ref, owners_ref, new_in, upd_in, new_ref, upd_ref, norm_ref, tails, sem):
    shard, short = new_in.shape[1:]
    copies = (
        pltpu.make_async_copy(upd_in.at[:, pl.ds(shard, EXTRA)], tails, sem.at[0]),
        pltpu.make_async_copy(new_in, new_ref, sem.at[1]),
        pltpu.make_async_copy(upd_in.at[:, pl.ds(0, shard)], upd_ref, sem.at[2]),
    )
    for copy in copies:
        copy.start()
    me = lax.axis_index("zero")
    copies[0].wait()
    result = jnp.zeros((1, short), F32)
    for k in range(mats):
        area = (shapes_ref[0, k] * shapes_ref[1, k]).astype(F32)
        norm = jnp.sum(tails[k].astype(F32), axis=0, keepdims=True)
        held = jnp.full((1, short), owners_ref[k], jnp.int32) == me
        result = result + jnp.where(held, norm / jnp.sqrt(jnp.full((1, short), area, F32)), 0.0)
    norm_ref[...] = result[:, 0:1]
    copies[1].wait()
    copies[2].wait()


def per_device(n_dp, n_zero, grad_partial, momentum, shapes, owners):
    mats, shard, short = momentum.shape
    smem = pl.BlockSpec(memory_space=pltpu.SMEM)
    hbm = pl.BlockSpec(memory_space=pltpu.HBM)
    anywhere = pl.BlockSpec(memory_space=pl.ANY)
    slots = 9
    turned = pltpu.with_memory_space_constraint(shapes.T, pltpu.HBM)
    owners = pltpu.with_memory_space_constraint(owners, pltpu.HBM)
    new, update = pl.pallas_call(
        functools.partial(kernel, mats, n_dp, n_zero),
        out_shape=(
            jax.ShapeDtypeStruct((mats, shard, short), F32),
            jax.ShapeDtypeStruct((mats, shard + EXTRA, short), BF16),
        ),
        in_specs=[smem, hbm, hbm],
        out_specs=(anywhere, anywhere),
        scratch_shapes=[
            pltpu.VMEM((mats, shard, short), BF16),
            pltpu.VMEM((mats, shard, short), F32),
            pltpu.VMEM((mats, shard, short), BF16),
            pltpu.VMEM((mats, shard, short), F32),
            pltpu.VMEM((shard + EXTRA, short), BF16),
            pltpu.VMEM((2, slots, PARTS[0][1], short), BF16),
            pltpu.VMEM((2, slots, PARTS[1][1], short), BF16),
            pltpu.VMEM((2, slots, PARTS[0][1], short), BF16),
            pltpu.VMEM((2, slots, PARTS[1][1], short), BF16),
            pltpu.VMEM((128, short), BF16),
            pltpu.VMEM((short, short), F32),
            pltpu.VMEM((n_zero, short // n_zero, short), F32),
            pltpu.VMEM((short, short), F32),
            pltpu.SemaphoreType.DMA((2,)),
            pltpu.SemaphoreType.DMA((2,)),
            pltpu.SemaphoreType.REGULAR((4,)),
            pltpu.SemaphoreType.DMA((len(PARTS), 2, slots)),
            pltpu.SemaphoreType.DMA((len(PARTS), 2, slots)),
            pltpu.SemaphoreType.DMA((2, len(PARTS), 2, slots)),
            pltpu.SemaphoreType.DMA((2, len(PARTS), 2, slots)),
            pltpu.SemaphoreType.DMA((2,)),
            pltpu.SemaphoreType.DMA((2,)),
        ],
        compiler_params=pltpu.CompilerParams(
            collective_id=0, has_side_effects=True, vmem_limit_bytes=24 * 1024 * 1024
        ),
    )(turned, *(pltpu.with_memory_space_constraint(a, pltpu.HBM) for a in (grad_partial, momentum)))
    return pl.pallas_call(
        functools.partial(finish, mats),
        out_shape=(
            jax.ShapeDtypeStruct((mats, shard, short), F32),
            jax.ShapeDtypeStruct((mats, shard, short), BF16),
            jax.ShapeDtypeStruct((1, 1), F32),
        ),
        in_specs=[smem, smem, anywhere, anywhere],
        out_specs=(anywhere, anywhere, pl.BlockSpec(memory_space=pltpu.VMEM)),
        scratch_shapes=[pltpu.VMEM((mats, EXTRA, short), BF16), pltpu.SemaphoreType.DMA((3,))],
        compiler_params=pltpu.CompilerParams(vmem_limit_bytes=24 * 1024 * 1024),
    )(turned, owners, new, update)


def solution(mesh):
    in_specs = (P("dp", None, "zero", None), P(None, "zero", None), P(), P())
    out_specs = (P(None, "zero", None), P(None, "zero", None), P("zero", None))
    return jax.shard_map(
        functools.partial(per_device, mesh.shape["dp"], mesh.shape["zero"]),
        mesh=mesh, in_specs=in_specs, out_specs=out_specs, check_vma=False,
    )
```

```python
import functools

import jax
import jax.numpy as jnp
from jax import lax
from jax.experimental import pallas as pl
from jax.experimental.pallas import tpu as pltpu
from jax.sharding import PartitionSpec as P

ITERS = 3
coef_a = 3.4445
coef_b = -4.775
coef_c = 2.0315
epsilon = 1e-07
momentum_decay = 0.95

MESH = pl.DeviceIdType.MESH
F32, BF16 = jnp.float32, jnp.bfloat16

PARENT = {8: 6, 7: 6, 6: 4, 5: 4, 4: 2, 3: 2, 2: 0, 1: 0}
SIDES = (1, -1)
PARTS = ((0, 64, (8, 7)), (64, 48, (7, 8)))
SIDE_X, SIDE_Y = 4, 4
EXTRA = 16


def children(node, reach):
    return [c for c in sorted(PARENT, reverse=True) if PARENT[c] == node and c <= reach]


def split(value):
    high = value.astype(BF16)
    return high, (value - high.astype(F32)).astype(BF16)


def dot(a, b):
    return jnp.dot(a, b, preferred_element_type=F32)


def chip_moves():
    def far(step, size):
        return min(step, size - step)

    moves = [(y, x) for y in range(SIDE_Y) for x in range(SIDE_X)]
    return sorted(moves, key=lambda m: -(far(m[0], SIDE_Y) + far(m[1], SIDE_X)))


def kernel(
    mats, n_dp, n_zero, shapes_ref, owners_ref, grad_ref, mom_ref, new_ref, upd_ref, norm_ref,
    grads, moms, sums, news, own, tails, arrived_a, arrived_b, outgoing_a, outgoing_b, nest, gram, slabs, whole,
    load_sem, store_sem, met_sem, rs_send, rs_recv, ag_send, ag_recv, plane_send, plane_recv,
):
    layer = lax.axis_index("dp")
    me = lax.axis_index("zero")
    shard, short = grads.shape[1:]
    half_short = short // 2
    slab = 3 * half_short // (SIDE_X * SIDE_Y)
    arrived, outgoing = (arrived_a, arrived_b), (outgoing_a, outgoing_b)
    half = n_dp // 2

    def held(at):
        return (at - (half - 1)) * (at - half) != 0

    def matrix(at):
        return at - (n_dp - mats) * (at // half)

    owner = held(layer)
    mine = matrix(layer)

    load_grads = pltpu.make_async_copy(grad_ref.at[0], grads, load_sem.at[0])
    load_grads.start()
    load_moms = pltpu.make_async_copy(mom_ref, moms, load_sem.at[1])
    load_moms.start()

    def along(step):
        return lax.rem(layer + (step + n_dp), n_dp)

    core, here_x, here_y = lax.rem(me, 2), lax.rem(me // 2, SIDE_X), me // (2 * SIDE_X)

    def beside(move):
        y, x, c = move
        there_y = lax.rem(here_y + (y + SIDE_Y), SIDE_Y)
        there_x = lax.rem(here_x + (x + SIDE_X), SIDE_X)
        return (there_y * SIDE_X + there_x) * 2 + lax.rem(core + c, 2)

    adds = core == lax.rem(here_x + here_y, 2)

    def adder(move):
        y, x = lax.rem(here_y + move[0], SIDE_Y), lax.rem(here_x + move[1], SIDE_X)
        chip = y * SIDE_X + x
        return chip, chip * 2 + lax.rem(x + y, 2)

    def greet(semaphore, where):
        pl.semaphore_signal(semaphore, inc=1, device_id=where, device_id_type=MESH)

    barrier = pltpu.get_barrier_semaphore()
    hops = sorted({c - p for c, p in PARENT.items()})
    for hop in hops:
        for side in SIDES:
            greet(barrier, {"dp": along(side * hop)})
    rows_x, rows_y, pair = ((0, 1, 0), (0, -1, 0)), ((1, 0, 0), (-1, 0, 0)), ((0, 0, 1),)
    for move in rows_x + rows_y + pair:
        greet(barrier, {"zero": beside(move)})
    load_grads.wait()
    pl.semaphore_wait(barrier, 2 * len(hops) + 5)
    rounds = (rows_x, pair, rows_y, ((1, 0, 0),))

    def meet(index):
        if index > 0:
            pl.semaphore_wait(met_sem.at[index - 1], len(rounds[index - 1]))
        if index < len(rounds):
            for move in rounds[index]:
                greet(met_sem.at[index], {"zero": beside(move)})

    meet(0)

    def reduce_copy(part, s, node, source):
        return pltpu.make_async_remote_copy(
            src_ref=source,
            dst_ref=arrived[part].at[s, node],
            send_sem=rs_send.at[part, s, node],
            recv_sem=rs_recv.at[part, s, node],
            device_id={"dp": along(SIDES[s] * (node - PARENT[node]))},
            device_id_type=MESH,
        )

    def own_rows(part, j):
        first, rows, _ = PARTS[part]
        return grads.at[matrix(j), pl.ds(first, rows)]

    def collected(part, s, node, total):
        for child in reversed(children(node, PARTS[part][2][s])):
            reduce_copy(part, s, child, arrived[part].at[s, child]).wait_recv()
            total = total + arrived[part][s, child].astype(F32)
        return total

    def reduce_source(part, s, node, j):
        if children(node, PARTS[part][2][s]):
            return outgoing[part].at[s, node]
        return own_rows(part, j)

    def reduce_step(node):
        for part in range(len(PARTS)):
            for s, side in enumerate(SIDES):
                if node > PARTS[part][2][s]:
                    continue
                j = along(side * node)

                @pl.when(held(j))
                def _():
                    if children(node, PARTS[part][2][s]):
                        total = collected(part, s, node, own_rows(part, j)[...].astype(F32))
                        outgoing[part][s, node] = total.astype(BF16)
                    reduce_copy(part, s, node, reduce_source(part, s, node, j)).start()

    for node in (8, 7, 5, 6):
        reduce_step(node)
    meet(1)
    for node in (3, 4):
        reduce_step(node)
    meet(2)
    for node in (1, 2):
        reduce_step(node)
    meet(3)

    def spread_copy(which, part, s, node, j):
        first, rows, _ = PARTS[part]
        if which == 1 and part == len(PARTS) - 1:
            rows += EXTRA
        window = (sums, upd_ref)[which].at[matrix(j), pl.ds(first, rows)]
        source = window
        if which == 1 and PARENT[node] == 0:
            source = own.at[pl.ds(first, rows)]
        return pltpu.make_async_remote_copy(
            src_ref=source,
            dst_ref=window,
            send_sem=ag_send.at[which, part, s, node],
            recv_sem=ag_recv.at[which, part, s, node],
            device_id={"dp": along(SIDES[s] * (node - PARENT[node]))},
            device_id_type=MESH,
        )

    def spread_step(which, node):
        for leaf in (False, True):
            for part in range(len(PARTS)):
                for s, side in enumerate(SIDES):
                    reach = PARTS[part][2][s]
                    targets = [c for c in children(node, reach) if (not children(c, reach)) == leaf]
                    if node > reach or (leaf and not targets):
                        continue
                    j = along(-side * node)

                    @pl.when(held(j))
                    def _():
                        if node > 0 and (not leaf or not children(node, reach)):
                            spread_copy(which, part, s, node, j).wait_recv()
                        for child in targets:
                            spread_copy(which, part, s, child, j).start()

    def spread_sent(which):
        for node in PARENT:
            for s, side in enumerate(SIDES):
                j = along(-side * PARENT[node])

                @pl.when(held(j))
                def _():
                    for part in range(len(PARTS)):
                        if node <= PARTS[part][2][s]:
                            spread_copy(which, part, s, node, j).wait_send()

    def plane_copy(source, target, which, peer):
        return pltpu.make_async_remote_copy(
            src_ref=source,
            dst_ref=target,
            send_sem=plane_send.at[which],
            recv_sem=plane_recv.at[which],
            device_id={"zero": peer},
            device_id_type=MESH,
        )

    def slab_of(ref, index):
        return ref.at[pl.ds(pl.multiple_of(index * slab, slab), slab)]

    def plane_wait(which, count):
        view = slabs.at[pl.ds(0, count)]
        return plane_copy(view, view, which, lax.rem(me + 1, n_zero))

    row_ids = me * shard + lax.broadcasted_iota(jnp.int32, (shard, short), 0)
    col_ids = lax.broadcasted_iota(jnp.int32, (shard, short), 1)

    def live_part(j):
        return (row_ids < shapes_ref[0, j]) & (col_ids < shapes_ref[1, j])

    def new_momentum(j, gradient):
        news[j] = jnp.where(live_part(j), momentum_decay * moms[j] + gradient, 0.0)

    load_moms.wait()
    meet(4)

    @pl.when(owner)
    def _():
        totals = []
        for part in range(len(PARTS)):
            total = own_rows(part, layer)[...].astype(F32)
            for s in range(2):
                total = collected(part, s, 0, total)
            totals.append(total)
        live = live_part(mine)
        gradient = jnp.where(live, jnp.concatenate(totals, axis=0), 0.0)
        sums[mine] = gradient.astype(BF16)
        momentum = jnp.where(live, momentum_decay * moms[mine] + gradient, 0.0)
        nesterov = (gradient + momentum_decay * momentum).astype(BF16)
        nest[0:shard] = nesterov
        nest[shard:] = jnp.zeros((nest.shape[0] - shard, short), BF16)
        left, right = nest[:, 0:half_short], nest[:, half_short:]
        for index, (a, b) in enumerate(((left, left), (left, right), (right, right))):
            gram[pl.ds(index * half_short, half_short)] = lax.dot_general(
                a, b, (((0,), (0,)), ((), ())), preferred_element_type=F32
            )
        for move in chip_moves()[:-1]:
            chip, peer = adder(move)
            plane_copy(slab_of(gram, chip), slabs.at[me], 0, peer).start()

        @pl.when(adds)
        def _():
            slabs[me] = slab_of(gram, me // 2)[...]

        @pl.when(jnp.logical_not(adds))
        def _():
            plane_copy(slab_of(gram, me // 2), slabs.at[me], 0, beside((0, 0, 1))).start()

    spread_step(0, 0)
    spread_step(0, 2)

    @pl.when(owner)
    def _():
        @pl.when(adds)
        def _():
            plane_wait(0, n_zero - 1).wait_recv()
            mine_of = slab_of(whole, me // 2)
            mine_of[...] = jnp.sum(slabs[...], axis=0)
            for y, x in chip_moves():
                for c in (0, 1):
                    if (y, x, c) != (0, 0, 0):
                        plane_copy(mine_of, mine_of, 1, beside((y, x, c))).start()

    spread_step(0, 4)

    @pl.when(owner)
    def _():
        chips = n_zero // 2

        @pl.when(adds)
        def _():
            plane_wait(1, chips - 1).wait_recv()

        @pl.when(jnp.logical_not(adds))
        def _():
            plane_wait(1, chips).wait_recv()

        blocks = [whole[pl.ds(index * half_short, half_short)] for index in range(3)]
        full = jnp.concatenate(
            [jnp.concatenate(blocks[0:2], axis=1), jnp.concatenate([blocks[1].T, blocks[2]], axis=1)], axis=0
        )
        on_diagonal = lax.broadcasted_iota(jnp.int32, (short, short), 0) == lax.broadcasted_iota(
            jnp.int32, (short, short), 1
        )
        square = jnp.where(on_diagonal, full, 0.0)
        square = jnp.sum(jnp.sum(square, axis=0, keepdims=True), axis=1, keepdims=True)
        norm = jnp.sqrt(square)
        inverse = 1.0 / (norm + epsilon)
        a = full * (inverse * inverse)
        state = (nest[...].astype(F32) * inverse).astype(BF16)
        for sweep in range(ITERS):
            a_high, a_low = split(a)
            poly = (coef_b * a_high.astype(F32) + coef_c * dot(a_high, a_high)).astype(BF16)
            if sweep < ITERS - 1:
                half = coef_a * a + dot(a_high, poly) + dot(a_low, poly)
                half_high, half_low = split(half)
                a = coef_a * half + dot(poly, half_high) + dot(poly, half_low)
            state = (coef_a * state.astype(F32) + dot(state, poly)).astype(BF16)
        longest = jnp.maximum(shapes_ref[0, mine], shapes_ref[1, mine]).astype(F32)
        scale = 0.2 * jnp.sqrt(jnp.full((1, 1), longest, F32))
        own[0:shard] = (state[0:shard].astype(F32) * scale).astype(BF16)
        one = jnp.broadcast_to(norm, (EXTRA, short))
        high, rest = split(one)
        low, rest = split(one - high.astype(F32))
        place = lax.broadcasted_iota(jnp.int32, (EXTRA, short), 0)
        own[shard:] = jnp.where(
            place == 0, high.astype(F32), jnp.where(place == 1, low.astype(F32), jnp.where(place == 2, rest.astype(F32), 0.0))
        ).astype(BF16)

    spread_step(1, 0)
    keep = pltpu.make_async_copy(own, upd_ref.at[mine], store_sem.at[0])

    @pl.when(owner)
    def _():
        keep.start()

    def new_momenta(node):
        if node == 8:
            j = along(8)

            @pl.when(held(j))
            def _():
                new_momentum(matrix(j), sums[matrix(j)].astype(F32))
            return
        for s, side in enumerate(SIDES):
            if node == 0 and s == 1:
                continue
            j = along(-side * node)

            @pl.when(held(j))
            def _():
                new_momentum(matrix(j), sums[matrix(j)].astype(F32))

    spread_step(1, 2)
    spread_step(0, 6)
    spread_step(1, 4)
    spread_step(1, 6)
    for node in (1, 3, 5, 7, 8):
        spread_step(0, node)
    for node in range(9):
        new_momenta(node)
    store_news = pltpu.make_async_copy(news, new_ref, store_sem.at[1])
    store_news.start()

    for node in PARENT:
        for s, side in enumerate(SIDES):
            j = along(side * node)

            @pl.when(held(j))
            def _():
                for part in range(len(PARTS)):
                    if node <= PARTS[part][2][s]:
                        reduce_copy(part, s, node, reduce_source(part, s, node, j)).wait_send()

    spread_sent(0)

    @pl.when(owner)
    def _():
        keep.wait()

        @pl.when(adds)
        def _():
            plane_wait(0, n_zero // 2 - 1).wait_send()
            plane_wait(1, n_zero - 1).wait_send()

        @pl.when(jnp.logical_not(adds))
        def _():
            plane_wait(0, n_zero // 2).wait_send()

    for node in (1, 3, 5, 7, 8):
        spread_step(1, node)
    load_tails = pltpu.make_async_copy(upd_ref.at[:, pl.ds(shard, EXTRA)], tails, load_sem.at[0])
    load_tails.start()
    spread_sent(1)
    load_tails.wait()
    result = jnp.zeros((1, short), F32)
    for k in range(mats):
        area = (shapes_ref[0, k] * shapes_ref[1, k]).astype(F32)
        norm = jnp.sum(tails[k].astype(F32), axis=0, keepdims=True)
        kept = jnp.full((1, short), owners_ref[k], jnp.int32) == me
        result = result + jnp.where(kept, norm / jnp.sqrt(jnp.full((1, short), area, F32)), 0.0)
    norm_ref[...] = jnp.broadcast_to(result[:, 0 : norm_ref.shape[1]], norm_ref.shape)
    store_news.wait()


def finish(new_in, upd_in, norm_in, new_ref, upd_ref, norm_ref, sem):
    copies = (
        pltpu.make_async_copy(new_in, new_ref, sem.at[0]),
        pltpu.make_async_copy(upd_in.at[:, pl.ds(0, upd_ref.shape[1])], upd_ref, sem.at[1]),
    )
    for copy in copies:
        copy.start()
    norm_ref[...] = norm_in[0:1, 0:1]
    for copy in copies:
        copy.wait()


def per_device(n_dp, n_zero, grad_partial, momentum, shapes, owners):
    mats, shard, short = momentum.shape
    smem = pl.BlockSpec(memory_space=pltpu.SMEM)
    vmem = pl.BlockSpec(memory_space=pltpu.VMEM)
    hbm = pl.BlockSpec(memory_space=pltpu.HBM)
    anywhere = pl.BlockSpec(memory_space=pl.ANY)
    slots = 9
    turned = pltpu.with_memory_space_constraint(shapes.T, pltpu.HBM)
    owners = pltpu.with_memory_space_constraint(owners, pltpu.HBM)
    new, update, norms = pl.pallas_call(
        functools.partial(kernel, mats, n_dp, n_zero),
        out_shape=(
            jax.ShapeDtypeStruct((mats, shard, short), F32),
            jax.ShapeDtypeStruct((mats, shard + EXTRA, short), BF16),
            jax.ShapeDtypeStruct((8, 128), F32),
        ),
        in_specs=[smem, smem, hbm, hbm],
        out_specs=(anywhere, anywhere, vmem),
        scratch_shapes=[
            pltpu.VMEM((mats, shard, short), BF16),
            pltpu.VMEM((mats, shard, short), F32),
            pltpu.VMEM((mats, shard, short), BF16),
            pltpu.VMEM((mats, shard, short), F32),
            pltpu.VMEM((shard + EXTRA, short), BF16),
            pltpu.VMEM((mats, EXTRA, short), BF16),
            pltpu.VMEM((2, slots, PARTS[0][1], short), BF16),
            pltpu.VMEM((2, slots, PARTS[1][1], short), BF16),
            pltpu.VMEM((2, slots, PARTS[0][1], short), BF16),
            pltpu.VMEM((2, slots, PARTS[1][1], short), BF16),
            pltpu.VMEM((128, short), BF16),
            pltpu.VMEM((3 * short // 2, short // 2), F32),
            pltpu.VMEM((n_zero, 3 * short // n_zero, short // 2), F32),
            pltpu.VMEM((3 * short // 2, short // 2), F32),
            pltpu.SemaphoreType.DMA((2,)),
            pltpu.SemaphoreType.DMA((2,)),
            pltpu.SemaphoreType.REGULAR((4,)),
            pltpu.SemaphoreType.DMA((len(PARTS), 2, slots)),
            pltpu.SemaphoreType.DMA((len(PARTS), 2, slots)),
            pltpu.SemaphoreType.DMA((2, len(PARTS), 2, slots)),
            pltpu.SemaphoreType.DMA((2, len(PARTS), 2, slots)),
            pltpu.SemaphoreType.DMA((2,)),
            pltpu.SemaphoreType.DMA((2,)),
        ],
        compiler_params=pltpu.CompilerParams(
            collective_id=0, has_side_effects=True, vmem_limit_bytes=24 * 1024 * 1024
        ),
    )(turned, owners, *(pltpu.with_memory_space_constraint(a, pltpu.HBM) for a in (grad_partial, momentum)))
    return pl.pallas_call(
        finish,
        out_shape=(
            jax.ShapeDtypeStruct((mats, shard, short), F32),
            jax.ShapeDtypeStruct((mats, shard, short), BF16),
            jax.ShapeDtypeStruct((1, 1), F32),
        ),
        in_specs=[anywhere, anywhere, vmem],
        out_specs=(anywhere, anywhere, vmem),
        scratch_shapes=[pltpu.SemaphoreType.DMA((2,))],
        compiler_params=pltpu.CompilerParams(vmem_limit_bytes=24 * 1024 * 1024),
    )(new, update, norms)


def solution(mesh):
    in_specs = (P("dp", None, "zero", None), P(None, "zero", None), P(), P())
    out_specs = (P(None, "zero", None), P(None, "zero", None), P("zero", None))
    return jax.shard_map(
        functools.partial(per_device, mesh.shape["dp"], mesh.shape["zero"]),
        mesh=mesh, in_specs=in_specs, out_specs=out_specs, check_vma=False,
    )
```

```python
import functools

import jax
import jax.numpy as jnp
from jax import lax
from jax.experimental import pallas as pl
from jax.experimental.pallas import tpu as pltpu
from jax.sharding import PartitionSpec as P

ITERS = 3
coef_a = 3.4445
coef_b = -4.775
coef_c = 2.0315
epsilon = 1e-07
momentum_decay = 0.95

MESH = pl.DeviceIdType.MESH
F32, BF16 = jnp.float32, jnp.bfloat16

PARENT = {8: 6, 7: 6, 6: 4, 5: 4, 4: 2, 3: 2, 2: 0, 1: 0}
SIDES = (1, -1)
PARTS = ((0, 64, (8, 7)), (64, 48, (7, 8)))
SIDE_X, SIDE_Y = 4, 4


def children(node, reach):
    return [c for c in sorted(PARENT, reverse=True) if PARENT[c] == node and c <= reach]


def split(value):
    high = value.astype(BF16)
    return high, (value - high.astype(F32)).astype(BF16)


def dot(a, b):
    return jnp.dot(a, b, preferred_element_type=F32)


def chip_moves():
    def far(step, size):
        return min(step, size - step)

    moves = [(y, x) for y in range(SIDE_Y) for x in range(SIDE_X)]
    return sorted(moves, key=lambda m: -(far(m[0], SIDE_Y) + far(m[1], SIDE_X)))


def kernel(
    mats, n_dp, n_zero, shapes_ref, owners_ref, grad_ref, mom_ref, new_ref, upd_ref, norm_ref,
    grads, moms, sums, news, own, tiles, arrived, outgoing, nest, gram, slabs, whole,
    load_sem, store_sem, met_sem, rs_send, rs_recv, ag_send, ag_recv, plane_send, plane_recv,
):
    layer = lax.axis_index("dp")
    me = lax.axis_index("zero")
    shard, short = grads.shape[1:]
    half_short = short // 2
    slab = 3 * half_short // (SIDE_X * SIDE_Y)
    half = n_dp // 2

    def held(at):
        return (at - (half - 1)) * (at - half) != 0

    def matrix(at):
        return at - (n_dp - mats) * (at // half)

    owner = held(layer)
    mine = matrix(layer)

    load_grads = pltpu.make_async_copy(grad_ref.at[0], grads, load_sem.at[0])
    load_grads.start()
    load_moms = pltpu.make_async_copy(mom_ref, moms, load_sem.at[1])
    load_moms.start()

    def along(step):
        return lax.rem(layer + (step + n_dp), n_dp)

    core, here_x, here_y = lax.rem(me, 2), lax.rem(me // 2, SIDE_X), me // (2 * SIDE_X)

    def beside(move):
        y, x, c = move
        there_y = lax.rem(here_y + (y + SIDE_Y), SIDE_Y)
        there_x = lax.rem(here_x + (x + SIDE_X), SIDE_X)
        return (there_y * SIDE_X + there_x) * 2 + lax.rem(core + c, 2)

    adds = core == lax.rem(here_x + here_y, 2)

    def adder(move):
        y, x = lax.rem(here_y + move[0], SIDE_Y), lax.rem(here_x + move[1], SIDE_X)
        chip = y * SIDE_X + x
        return chip, chip * 2 + lax.rem(x + y, 2)

    def greet(semaphore, where):
        pl.semaphore_signal(semaphore, inc=1, device_id=where, device_id_type=MESH)

    barrier = pltpu.get_barrier_semaphore()
    hops = sorted({c - p for c, p in PARENT.items()})
    for hop in hops:
        for side in SIDES:
            greet(barrier, {"dp": along(side * hop)})
    rows_x, rows_y, pair = ((0, 1, 0), (0, -1, 0)), ((1, 0, 0), (-1, 0, 0)), ((0, 0, 1),)
    for move in rows_x + rows_y + pair:
        greet(barrier, {"zero": beside(move)})
    load_grads.wait()
    pl.semaphore_wait(barrier, 2 * len(hops) + 5)
    rounds = (rows_x, pair, rows_y, ((1, 0, 0),))

    def meet(index):
        if index > 0:
            pl.semaphore_wait(met_sem.at[index - 1], len(rounds[index - 1]))
        if index < len(rounds):
            for move in rounds[index]:
                greet(met_sem.at[index], {"zero": beside(move)})

    meet(0)

    def block(ref, part, *where):
        first, rows, _ = PARTS[part]
        return ref.at[*where, pl.ds(first, rows)]

    def reduce_copy(part, s, node, source):
        return pltpu.make_async_remote_copy(
            src_ref=source,
            dst_ref=block(arrived, part, s, node),
            send_sem=rs_send.at[part, s, node],
            recv_sem=rs_recv.at[part, s, node],
            device_id={"dp": along(SIDES[s] * (node - PARENT[node]))},
            device_id_type=MESH,
        )

    def own_rows(part, j):
        return block(grads, part, matrix(j))

    def collected(part, s, node, total):
        for child in reversed(children(node, PARTS[part][2][s])):
            reduce_copy(part, s, child, block(arrived, part, s, child)).wait_recv()
            total = total + block(arrived, part, s, child)[...].astype(F32)
        return total

    def reduce_source(part, s, node, j):
        if children(node, PARTS[part][2][s]):
            return block(outgoing, part, s, node)
        return own_rows(part, j)

    def reduce_step(node):
        for part in range(len(PARTS)):
            for s, side in enumerate(SIDES):
                if node > PARTS[part][2][s]:
                    continue
                j = along(side * node)

                @pl.when(held(j))
                def _():
                    if children(node, PARTS[part][2][s]):
                        total = collected(part, s, node, own_rows(part, j)[...].astype(F32))
                        block(outgoing, part, s, node)[...] = total.astype(BF16)
                    reduce_copy(part, s, node, reduce_source(part, s, node, j)).start()

    for node in (8, 7, 5, 6):
        reduce_step(node)
    meet(1)
    for node in (3, 4):
        reduce_step(node)
    meet(2)
    for node in (1, 2):
        reduce_step(node)
    meet(3)

    def spread_copy(which, part, s, node, j):
        first, rows, _ = PARTS[part]
        window = (sums, upd_ref)[which].at[matrix(j), pl.ds(first, rows)]
        source = window
        if which == 1 and PARENT[node] == 0:
            source = own.at[pl.ds(first, rows)]
        return pltpu.make_async_remote_copy(
            src_ref=source,
            dst_ref=window,
            send_sem=ag_send.at[which, part, s, node],
            recv_sem=ag_recv.at[which, part, s, node],
            device_id={"dp": along(SIDES[s] * (node - PARENT[node]))},
            device_id_type=MESH,
        )

    def spread_step(which, node):
        for leaf in (False, True):
            for part in range(len(PARTS)):
                for s, side in enumerate(SIDES):
                    reach = PARTS[part][2][s]
                    targets = [c for c in children(node, reach) if (not children(c, reach)) == leaf]
                    if node > reach or (leaf and not targets):
                        continue
                    j = along(-side * node)

                    @pl.when(held(j))
                    def _():
                        if node > 0 and (not leaf or not children(node, reach)):
                            spread_copy(which, part, s, node, j).wait_recv()
                        for child in targets:
                            spread_copy(which, part, s, child, j).start()

    def spread_sent(which):
        for node in PARENT:
            for s, side in enumerate(SIDES):
                j = along(-side * PARENT[node])

                @pl.when(held(j))
                def _():
                    for part in range(len(PARTS)):
                        if node <= PARTS[part][2][s]:
                            spread_copy(which, part, s, node, j).wait_send()

    def plane_copy(source, target, which, peer):
        return pltpu.make_async_remote_copy(
            src_ref=source,
            dst_ref=target,
            send_sem=plane_send.at[which],
            recv_sem=plane_recv.at[which],
            device_id={"zero": peer},
            device_id_type=MESH,
        )

    def slab_of(ref, index):
        return ref.at[pl.ds(pl.multiple_of(index * slab, slab), slab)]

    def plane_wait(which, count):
        view = slabs.at[pl.ds(0, count)]
        return plane_copy(view, view, which, lax.rem(me + 1, n_zero))

    row_ids = me * shard + lax.broadcasted_iota(jnp.int32, (shard, short), 0)
    col_ids = lax.broadcasted_iota(jnp.int32, (shard, short), 1)

    def live_part(j):
        return (row_ids < shapes_ref[0, j]) & (col_ids < shapes_ref[1, j])

    def new_momentum(j, gradient):
        news[j] = jnp.where(live_part(j), momentum_decay * moms[j] + gradient, 0.0)

    load_moms.wait()
    meet(4)

    @pl.when(owner)
    def _():
        totals = []
        for part in range(len(PARTS)):
            total = own_rows(part, layer)[...].astype(F32)
            for s in range(2):
                total = collected(part, s, 0, total)
            totals.append(total)
        live = live_part(mine)
        gradient = jnp.where(live, jnp.concatenate(totals, axis=0), 0.0)
        sums[mine] = gradient.astype(BF16)
        momentum = jnp.where(live, momentum_decay * moms[mine] + gradient, 0.0)
        nesterov = (gradient + momentum_decay * momentum).astype(BF16)
        nest[0:shard] = nesterov
        nest[shard:] = jnp.zeros((nest.shape[0] - shard, short), BF16)
        left, right = nest[:, 0:half_short], nest[:, half_short:]
        for index, (a, b) in enumerate(((left, left), (left, right), (right, right))):
            gram[pl.ds(index * half_short, half_short)] = lax.dot_general(
                a, b, (((0,), (0,)), ((), ())), preferred_element_type=F32
            )
        for move in chip_moves()[:-1]:
            chip, peer = adder(move)
            plane_copy(slab_of(gram, chip), slabs.at[me], 0, peer).start()

        @pl.when(adds)
        def _():
            slabs[me] = slab_of(gram, me // 2)[...]

        @pl.when(jnp.logical_not(adds))
        def _():
            plane_copy(slab_of(gram, me // 2), slabs.at[me], 0, beside((0, 0, 1))).start()

    spread_step(0, 0)
    spread_step(0, 2)

    @pl.when(owner)
    def _():
        @pl.when(adds)
        def _():
            plane_wait(0, n_zero - 1).wait_recv()
            mine_of = slab_of(whole, me // 2)
            mine_of[...] = jnp.sum(slabs[...], axis=0)
            for y, x in chip_moves():
                for c in (0, 1):
                    if (y, x, c) != (0, 0, 0):
                        plane_copy(mine_of, mine_of, 1, beside((y, x, c))).start()

    spread_step(0, 4)
    spread_step(0, 6)

    @pl.when(owner)
    def _():
        chips = n_zero // 2

        @pl.when(adds)
        def _():
            plane_wait(1, chips - 1).wait_recv()

        @pl.when(jnp.logical_not(adds))
        def _():
            plane_wait(1, chips).wait_recv()

        blocks = [whole[pl.ds(index * half_short, half_short)] for index in range(3)]
        full = jnp.concatenate(
            [jnp.concatenate(blocks[0:2], axis=1), jnp.concatenate([blocks[1].T, blocks[2]], axis=1)], axis=0
        )
        on_diagonal = lax.broadcasted_iota(jnp.int32, (short, short), 0) == lax.broadcasted_iota(
            jnp.int32, (short, short), 1
        )
        square = jnp.where(on_diagonal, full, 0.0)
        square = jnp.sum(jnp.sum(square, axis=0, keepdims=True), axis=1, keepdims=True)
        norm = jnp.sqrt(square)
        inverse = 1.0 / (norm + epsilon)
        a = full * (inverse * inverse)
        state = (nest[...].astype(F32) * inverse).astype(BF16)
        for sweep in range(ITERS):
            a_high, a_low = split(a)
            poly = (coef_b * a_high.astype(F32) + coef_c * dot(a_high, a_high)).astype(BF16)
            if sweep < ITERS - 1:
                both = dot(jnp.concatenate([a_high, a_low, state], axis=0), poly)
                half = coef_a * a + both[0:short] + both[short : 2 * short]
                half_high, half_low = split(half)
                twice = dot(poly, jnp.concatenate([half_high, half_low], axis=1))
                a = coef_a * half + twice[:, 0:short] + twice[:, short:]
                moved = both[2 * short :]
            else:
                moved = dot(state, poly)
            state = (coef_a * state.astype(F32) + moved).astype(BF16)
        longest = jnp.maximum(shapes_ref[0, mine], shapes_ref[1, mine]).astype(F32)
        scale = 0.2 * jnp.sqrt(jnp.full((1, 1), longest, F32))
        own[...] = (state[0:shard].astype(F32) * scale).astype(BF16)

    spread_step(1, 0)
    keep = pltpu.make_async_copy(own, upd_ref.at[mine], store_sem.at[0])

    @pl.when(owner)
    def _():
        keep.start()

    def new_momenta(node):
        if node == 8:
            j = along(8)

            @pl.when(held(j))
            def _():
                new_momentum(matrix(j), sums[matrix(j)].astype(F32))
            return
        for s, side in enumerate(SIDES):
            if node == 0 and s == 1:
                continue
            j = along(-side * node)

            @pl.when(held(j))
            def _():
                new_momentum(matrix(j), sums[matrix(j)].astype(F32))

    spread_step(1, 2)
    for node in (1, 3, 5, 7, 8):
        spread_step(0, node)
    for node in range(9):
        new_momenta(node)
    lanes = lax.broadcasted_iota(jnp.int32, (8, 128), 1)
    squares = jnp.zeros((8, 128), F32)
    for k in range(mats):
        value = (sums[k].astype(F32) + momentum_decay * news[k]).astype(BF16).astype(F32)
        total = jnp.sum(jnp.sum(value * value, axis=0, keepdims=True), axis=1, keepdims=True)
        squares = jnp.where(lanes == k, total, squares)
    tiles[me] = squares
    spread_step(1, 4)
    for y, x in chip_moves():
        for c in (0, 1):
            if (y, x, c) != (0, 0, 0):
                plane_copy(tiles.at[me], tiles.at[me], 2, beside((y, x, c))).start()
    spread_step(1, 6)
    store_news = pltpu.make_async_copy(news, new_ref, store_sem.at[1])
    store_news.start()

    for node in PARENT:
        for s, side in enumerate(SIDES):
            j = along(side * node)

            @pl.when(held(j))
            def _():
                for part in range(len(PARTS)):
                    if node <= PARTS[part][2][s]:
                        reduce_copy(part, s, node, reduce_source(part, s, node, j)).wait_send()

    spread_sent(0)

    @pl.when(owner)
    def _():
        keep.wait()

        @pl.when(adds)
        def _():
            plane_wait(0, n_zero // 2 - 1).wait_send()
            plane_wait(1, n_zero - 1).wait_send()

        @pl.when(jnp.logical_not(adds))
        def _():
            plane_wait(0, n_zero // 2).wait_send()

    for node in (1, 3, 5, 7, 8):
        spread_step(1, node)
    tile_view = tiles.at[pl.ds(0, n_zero - 1)]
    tile_wait = plane_copy(tile_view, tile_view, 2, lax.rem(me + 1, n_zero))
    tile_wait.wait_recv()
    norms = jnp.sqrt(jnp.sum(tiles[...], axis=0))
    result = jnp.zeros((8, 128), F32)
    for k in range(mats):
        area = jnp.full((8, 128), (shapes_ref[0, k] * shapes_ref[1, k]).astype(F32), F32)
        kept = (jnp.full((8, 128), owners_ref[k], jnp.int32) == me) & (lanes == k)
        result = jnp.where(kept, norms / jnp.sqrt(area), result)
    norm_ref[...] = jnp.broadcast_to(jnp.sum(result, axis=1, keepdims=True), norm_ref.shape)
    tile_wait.wait_send()
    spread_sent(1)
    store_news.wait()


def finish(new_in, upd_in, norm_in, new_ref, upd_ref, norm_ref, sem):
    copies = (
        pltpu.make_async_copy(new_in, new_ref, sem.at[0]),
        pltpu.make_async_copy(upd_in, upd_ref, sem.at[1]),
    )
    for copy in copies:
        copy.start()
    norm_ref[...] = norm_in[0:1, 0:1]
    for copy in copies:
        copy.wait()


def per_device(n_dp, n_zero, grad_partial, momentum, shapes, owners):
    mats, shard, short = momentum.shape
    smem = pl.BlockSpec(memory_space=pltpu.SMEM)
    vmem = pl.BlockSpec(memory_space=pltpu.VMEM)
    hbm = pl.BlockSpec(memory_space=pltpu.HBM)
    anywhere = pl.BlockSpec(memory_space=pl.ANY)
    slots = 9
    turned = pltpu.with_memory_space_constraint(shapes.T, pltpu.HBM)
    owners = pltpu.with_memory_space_constraint(owners, pltpu.HBM)
    new, update, norms = pl.pallas_call(
        functools.partial(kernel, mats, n_dp, n_zero),
        out_shape=(
            jax.ShapeDtypeStruct((mats, shard, short), F32),
            jax.ShapeDtypeStruct((mats, shard, short), BF16),
            jax.ShapeDtypeStruct((8, 128), F32),
        ),
        in_specs=[smem, smem, hbm, hbm],
        out_specs=(anywhere, anywhere, vmem),
        scratch_shapes=[
            pltpu.VMEM((mats, shard, short), BF16),
            pltpu.VMEM((mats, shard, short), F32),
            pltpu.VMEM((mats, shard, short), BF16),
            pltpu.VMEM((mats, shard, short), F32),
            pltpu.VMEM((shard, short), BF16),
            pltpu.VMEM((n_zero, 8, 128), F32),
            pltpu.VMEM((2, slots, shard, short), BF16),
            pltpu.VMEM((2, slots, shard, short), BF16),
            pltpu.VMEM((128, short), BF16),
            pltpu.VMEM((3 * short // 2, short // 2), F32),
            pltpu.VMEM((n_zero, 3 * short // n_zero, short // 2), F32),
            pltpu.VMEM((3 * short // 2, short // 2), F32),
            pltpu.SemaphoreType.DMA((2,)),
            pltpu.SemaphoreType.DMA((2,)),
            pltpu.SemaphoreType.REGULAR((4,)),
            pltpu.SemaphoreType.DMA((len(PARTS), 2, slots)),
            pltpu.SemaphoreType.DMA((len(PARTS), 2, slots)),
            pltpu.SemaphoreType.DMA((2, len(PARTS), 2, slots)),
            pltpu.SemaphoreType.DMA((2, len(PARTS), 2, slots)),
            pltpu.SemaphoreType.DMA((3,)),
            pltpu.SemaphoreType.DMA((3,)),
        ],
        compiler_params=pltpu.CompilerParams(
            collective_id=0, has_side_effects=True, vmem_limit_bytes=24 * 1024 * 1024
        ),
    )(turned, owners, *(pltpu.with_memory_space_constraint(a, pltpu.HBM) for a in (grad_partial, momentum)))
    return pl.pallas_call(
        finish,
        out_shape=(
            jax.ShapeDtypeStruct((mats, shard, short), F32),
            jax.ShapeDtypeStruct((mats, shard, short), BF16),
            jax.ShapeDtypeStruct((1, 1), F32),
        ),
        in_specs=[anywhere, anywhere, vmem],
        out_specs=(anywhere, anywhere, vmem),
        scratch_shapes=[pltpu.SemaphoreType.DMA((2,))],
        compiler_params=pltpu.CompilerParams(vmem_limit_bytes=24 * 1024 * 1024),
    )(new, update, norms)


def solution(mesh):
    in_specs = (P("dp", None, "zero", None), P(None, "zero", None), P(), P())
    out_specs = (P(None, "zero", None), P(None, "zero", None), P("zero", None))
    return jax.shard_map(
        functools.partial(per_device, mesh.shape["dp"], mesh.shape["zero"]),
        mesh=mesh, in_specs=in_specs, out_specs=out_specs, check_vma=False,
    )
```

```python
import functools

import jax
import jax.numpy as jnp
from jax import lax
from jax.experimental import pallas as pl
from jax.experimental.pallas import tpu as pltpu
from jax.sharding import PartitionSpec as P

ITERS = 3
coef_a = 3.4445
coef_b = -4.775
coef_c = 2.0315
epsilon = 1e-07
momentum_decay = 0.95

MESH = pl.DeviceIdType.MESH
F32, BF16 = jnp.float32, jnp.bfloat16

PARENT = {8: 6, 7: 6, 6: 4, 5: 4, 4: 2, 3: 2, 2: 0, 1: 0}
SIDES = (1, -1)
PARTS = ((0, 64, (8, 7)), (64, 48, (7, 8)))
SIDE_X, SIDE_Y = 4, 4


def children(node, reach):
    return [c for c in sorted(PARENT, reverse=True) if PARENT[c] == node and c <= reach]


def split(value):
    high = value.astype(BF16)
    return high, (value - high.astype(F32)).astype(BF16)


def dot(a, b):
    return jnp.dot(a, b, preferred_element_type=F32)


def chip_moves():
    def far(step, size):
        return min(step, size - step)

    moves = [(y, x) for y in range(SIDE_Y) for x in range(SIDE_X)]
    return sorted(moves, key=lambda m: -(far(m[0], SIDE_Y) + far(m[1], SIDE_X)))


def kernel(
    mats, n_dp, n_zero, shapes_ref, owners_ref, grad_ref, mom_ref, new_ref, upd_ref, norm_ref,
    grads, moms, sums, news, own, tiles, arrived, outgoing, nest, gram, slabs, whole,
    load_sem, store_sem, met_sem, rs_send, rs_recv, ag_send, ag_recv, plane_send, plane_recv,
):
    layer = lax.axis_index("dp")
    me = lax.axis_index("zero")
    shard, short = grads.shape[1:]
    half_short = short // 2
    slab = 3 * half_short // (SIDE_X * SIDE_Y)
    half = n_dp // 2

    def held(at):
        return (at - (half - 1)) * (at - half) != 0

    def matrix(at):
        return at - (n_dp - mats) * (at // half)

    owner = held(layer)
    mine = matrix(layer)

    load_grads = pltpu.make_async_copy(grad_ref.at[0], grads, load_sem.at[0])
    load_grads.start()
    load_moms = pltpu.make_async_copy(mom_ref, moms, load_sem.at[1])
    load_moms.start()

    def along(step):
        return lax.rem(layer + (step + n_dp), n_dp)

    core, here_x, here_y = lax.rem(me, 2), lax.rem(me // 2, SIDE_X), me // (2 * SIDE_X)

    def beside(move):
        y, x, c = move
        there_y = lax.rem(here_y + (y + SIDE_Y), SIDE_Y)
        there_x = lax.rem(here_x + (x + SIDE_X), SIDE_X)
        return (there_y * SIDE_X + there_x) * 2 + lax.rem(core + c, 2)

    adds = core == lax.rem(here_x + here_y, 2)

    def adder(move):
        y, x = lax.rem(here_y + move[0], SIDE_Y), lax.rem(here_x + move[1], SIDE_X)
        chip = y * SIDE_X + x
        return chip, chip * 2 + lax.rem(x + y, 2)

    def greet(semaphore, where):
        pl.semaphore_signal(semaphore, inc=1, device_id=where, device_id_type=MESH)

    barrier = pltpu.get_barrier_semaphore()
    hops = sorted({c - p for c, p in PARENT.items()})
    for hop in hops:
        for side in SIDES:
            greet(barrier, {"dp": along(side * hop)})
    rows_x, rows_y, pair = ((0, 1, 0), (0, -1, 0)), ((1, 0, 0), (-1, 0, 0)), ((0, 0, 1),)
    for move in rows_x + rows_y + pair:
        greet(barrier, {"zero": beside(move)})
    load_grads.wait()
    pl.semaphore_wait(barrier, 2 * len(hops) + 5)
    rounds = (rows_x, pair, rows_y, ((1, 0, 0),))

    def meet(index):
        if index > 0:
            pl.semaphore_wait(met_sem.at[index - 1], len(rounds[index - 1]))
        if index < len(rounds):
            for move in rounds[index]:
                greet(met_sem.at[index], {"zero": beside(move)})

    meet(0)

    def block(ref, part, *where):
        first, rows, _ = PARTS[part]
        return ref.at[*where, pl.ds(first, rows)]

    def reduce_copy(part, s, node, source):
        return pltpu.make_async_remote_copy(
            src_ref=source,
            dst_ref=block(arrived, part, s, node),
            send_sem=rs_send.at[part, s, node],
            recv_sem=rs_recv.at[part, s, node],
            device_id={"dp": along(SIDES[s] * (node - PARENT[node]))},
            device_id_type=MESH,
        )

    def own_rows(part, j):
        return block(grads, part, matrix(j))

    def collected(part, s, node, total):
        for child in reversed(children(node, PARTS[part][2][s])):
            reduce_copy(part, s, child, block(arrived, part, s, child)).wait_recv()
            total = total + block(arrived, part, s, child)[...].astype(F32)
        return total

    def reduce_source(part, s, node, j):
        if children(node, PARTS[part][2][s]):
            return block(outgoing, part, s, node)
        return own_rows(part, j)

    def reduce_step(node, parts=tuple(range(len(PARTS)))):
        for part in parts:
            for s, side in enumerate(SIDES):
                if node > PARTS[part][2][s]:
                    continue
                j = along(side * node)

                @pl.when(held(j))
                def _():
                    if children(node, PARTS[part][2][s]):
                        total = collected(part, s, node, own_rows(part, j)[...].astype(F32))
                        block(outgoing, part, s, node)[...] = total.astype(BF16)
                    reduce_copy(part, s, node, reduce_source(part, s, node, j)).start()

    for part in range(len(PARTS)):
        for node in (8, 7):
            reduce_step(node, (part,))
    for node in (5, 6):
        reduce_step(node)
    meet(1)
    for node in (3, 4):
        reduce_step(node)
    meet(2)
    for node in (1, 2):
        reduce_step(node)
    meet(3)

    def spread_copy(which, part, s, node, j):
        first, rows, _ = PARTS[part]
        window = (sums, upd_ref)[which].at[matrix(j), pl.ds(first, rows)]
        source = window
        if which == 1 and PARENT[node] == 0:
            source = own.at[pl.ds(first, rows)]
        return pltpu.make_async_remote_copy(
            src_ref=source,
            dst_ref=window,
            send_sem=ag_send.at[which, part, s, node],
            recv_sem=ag_recv.at[which, part, s, node],
            device_id={"dp": along(SIDES[s] * (node - PARENT[node]))},
            device_id_type=MESH,
        )

    def spread_step(which, node):
        for leaf in (False, True):
            for part in range(len(PARTS)):
                for s, side in enumerate(SIDES):
                    reach = PARTS[part][2][s]
                    targets = [c for c in children(node, reach) if (not children(c, reach)) == leaf]
                    if node > reach or (leaf and not targets):
                        continue
                    j = along(-side * node)

                    @pl.when(held(j))
                    def _():
                        if node > 0 and (not leaf or not children(node, reach)):
                            spread_copy(which, part, s, node, j).wait_recv()
                        for child in targets:
                            spread_copy(which, part, s, child, j).start()

    def spread_sent(which):
        for node in PARENT:
            for s, side in enumerate(SIDES):
                j = along(-side * PARENT[node])

                @pl.when(held(j))
                def _():
                    for part in range(len(PARTS)):
                        if node <= PARTS[part][2][s]:
                            spread_copy(which, part, s, node, j).wait_send()

    def plane_copy(source, target, which, peer):
        return pltpu.make_async_remote_copy(
            src_ref=source,
            dst_ref=target,
            send_sem=plane_send.at[which],
            recv_sem=plane_recv.at[which],
            device_id={"zero": peer},
            device_id_type=MESH,
        )

    def slab_of(ref, index):
        return ref.at[pl.ds(pl.multiple_of(index * slab, slab), slab)]

    def plane_wait(which, count):
        view = slabs.at[pl.ds(0, count)]
        return plane_copy(view, view, which, lax.rem(me + 1, n_zero))

    row_ids = me * shard + lax.broadcasted_iota(jnp.int32, (shard, short), 0)
    col_ids = lax.broadcasted_iota(jnp.int32, (shard, short), 1)

    def live_part(j):
        return (row_ids < shapes_ref[0, j]) & (col_ids < shapes_ref[1, j])

    def new_momentum(j, gradient):
        news[j] = jnp.where(live_part(j), momentum_decay * moms[j] + gradient, 0.0)

    load_moms.wait()
    meet(4)

    @pl.when(owner)
    def _():
        totals = []
        for part in range(len(PARTS)):
            total = own_rows(part, layer)[...].astype(F32)
            for s in range(2):
                total = collected(part, s, 0, total)
            totals.append(total)
        live = live_part(mine)
        gradient = jnp.where(live, jnp.concatenate(totals, axis=0), 0.0)
        sums[mine] = gradient.astype(BF16)
        momentum = jnp.where(live, momentum_decay * moms[mine] + gradient, 0.0)
        nesterov = (gradient + momentum_decay * momentum).astype(BF16)
        nest[0:shard] = nesterov
        nest[shard:] = jnp.zeros((nest.shape[0] - shard, short), BF16)
        left, right = nest[:, 0:half_short], nest[:, half_short:]
        for index, (a, b) in enumerate(((left, left), (left, right), (right, right))):
            gram[pl.ds(index * half_short, half_short)] = lax.dot_general(
                a, b, (((0,), (0,)), ((), ())), preferred_element_type=F32
            )
        for move in chip_moves()[:-1]:
            chip, peer = adder(move)
            plane_copy(slab_of(gram, chip), slabs.at[me], 0, peer).start()

        @pl.when(adds)
        def _():
            slabs[me] = slab_of(gram, me // 2)[...]

        @pl.when(jnp.logical_not(adds))
        def _():
            plane_copy(slab_of(gram, me // 2), slabs.at[me], 0, beside((0, 0, 1))).start()

    spread_step(0, 0)
    spread_step(0, 2)

    @pl.when(owner)
    def _():
        @pl.when(adds)
        def _():
            plane_wait(0, n_zero - 1).wait_recv()
            mine_of = slab_of(whole, me // 2)
            mine_of[...] = jnp.sum(slabs[...], axis=0)
            for y, x in chip_moves():
                for c in (0, 1):
                    if (y, x, c) != (0, 0, 0):
                        plane_copy(mine_of, mine_of, 1, beside((y, x, c))).start()

    spread_step(0, 4)
    spread_step(0, 6)

    @pl.when(owner)
    def _():
        chips = n_zero // 2

        @pl.when(adds)
        def _():
            plane_wait(1, chips - 1).wait_recv()

        @pl.when(jnp.logical_not(adds))
        def _():
            plane_wait(1, chips).wait_recv()

        blocks = [whole[pl.ds(index * half_short, half_short)] for index in range(3)]
        full = jnp.concatenate(
            [jnp.concatenate(blocks[0:2], axis=1), jnp.concatenate([blocks[1].T, blocks[2]], axis=1)], axis=0
        )
        on_diagonal = lax.broadcasted_iota(jnp.int32, (short, short), 0) == lax.broadcasted_iota(
            jnp.int32, (short, short), 1
        )
        square = jnp.where(on_diagonal, full, 0.0)
        square = jnp.sum(jnp.sum(square, axis=0, keepdims=True), axis=1, keepdims=True)
        norm = jnp.sqrt(square)
        inverse = 1.0 / (norm + epsilon)
        a = full * (inverse * inverse)
        state = (nest[...].astype(F32) * inverse).astype(BF16)
        for sweep in range(ITERS):
            a_high, a_low = split(a)
            poly = (coef_b * a_high.astype(F32) + coef_c * dot(a_high, a_high)).astype(BF16)
            if sweep < ITERS - 1:
                both = dot(jnp.concatenate([a_high, a_low, state], axis=0), poly)
                half = coef_a * a + both[0:short] + both[short : 2 * short]
                half_high, half_low = split(half)
                twice = dot(poly, jnp.concatenate([half_high, half_low], axis=1))
                a = coef_a * half + twice[:, 0:short] + twice[:, short:]
                moved = both[2 * short :]
            else:
                moved = dot(state, poly)
            state = (coef_a * state.astype(F32) + moved).astype(BF16)
        longest = jnp.maximum(shapes_ref[0, mine], shapes_ref[1, mine]).astype(F32)
        scale = 0.2 * jnp.sqrt(jnp.full((1, 1), longest, F32))
        own[...] = (state[0:shard].astype(F32) * scale).astype(BF16)

    spread_step(1, 0)
    keep = pltpu.make_async_copy(own, upd_ref.at[mine], store_sem.at[0])

    @pl.when(owner)
    def _():
        keep.start()

    def new_momenta(node):
        if node == 8:
            j = along(8)

            @pl.when(held(j))
            def _():
                new_momentum(matrix(j), sums[matrix(j)].astype(F32))
            return
        for s, side in enumerate(SIDES):
            if node == 0 and s == 1:
                continue
            j = along(-side * node)

            @pl.when(held(j))
            def _():
                new_momentum(matrix(j), sums[matrix(j)].astype(F32))

    spread_step(1, 2)
    for node in (1, 3, 5, 7, 8):
        spread_step(0, node)
    for node in range(9):
        new_momenta(node)
    lanes = lax.broadcasted_iota(jnp.int32, (8, 128), 1)
    squares = jnp.zeros((8, 128), F32)
    for k in range(mats):
        value = (sums[k].astype(F32) + momentum_decay * news[k]).astype(BF16).astype(F32)
        total = jnp.sum(jnp.sum(value * value, axis=0, keepdims=True), axis=1, keepdims=True)
        squares = jnp.where(lanes == k, total, squares)
    tiles[me] = squares
    spread_step(1, 4)
    for y, x in chip_moves():
        for c in (0, 1):
            if (y, x, c) != (0, 0, 0):
                plane_copy(tiles.at[me], tiles.at[me], 2, beside((y, x, c))).start()
    spread_step(1, 6)
    store_news = pltpu.make_async_copy(news, new_ref, store_sem.at[1])
    store_news.start()

    for node in PARENT:
        for s, side in enumerate(SIDES):
            j = along(side * node)

            @pl.when(held(j))
            def _():
                for part in range(len(PARTS)):
                    if node <= PARTS[part][2][s]:
                        reduce_copy(part, s, node, reduce_source(part, s, node, j)).wait_send()

    spread_sent(0)

    @pl.when(owner)
    def _():
        keep.wait()

        @pl.when(adds)
        def _():
            plane_wait(0, n_zero // 2 - 1).wait_send()
            plane_wait(1, n_zero - 1).wait_send()

        @pl.when(jnp.logical_not(adds))
        def _():
            plane_wait(0, n_zero // 2).wait_send()

    for node in (1, 3, 5, 7, 8):
        spread_step(1, node)
    tile_view = tiles.at[pl.ds(0, n_zero - 1)]
    tile_wait = plane_copy(tile_view, tile_view, 2, lax.rem(me + 1, n_zero))
    tile_wait.wait_recv()
    norms = jnp.sqrt(jnp.sum(tiles[...], axis=0))
    result = jnp.zeros((8, 128), F32)
    for k in range(mats):
        area = jnp.full((8, 128), (shapes_ref[0, k] * shapes_ref[1, k]).astype(F32), F32)
        kept = (jnp.full((8, 128), owners_ref[k], jnp.int32) == me) & (lanes == k)
        result = jnp.where(kept, norms / jnp.sqrt(area), result)
    norm_ref[...] = jnp.broadcast_to(jnp.sum(result, axis=1, keepdims=True), norm_ref.shape)
    tile_wait.wait_send()
    spread_sent(1)
    store_news.wait()


def finish(new_in, upd_in, norm_in, new_ref, upd_ref, norm_ref, sem):
    copies = (
        pltpu.make_async_copy(new_in, new_ref, sem.at[0]),
        pltpu.make_async_copy(upd_in, upd_ref, sem.at[1]),
    )
    for copy in copies:
        copy.start()
    norm_ref[...] = norm_in[0:1, 0:1]
    for copy in copies:
        copy.wait()


def per_device(n_dp, n_zero, grad_partial, momentum, shapes, owners):
    mats, shard, short = momentum.shape
    smem = pl.BlockSpec(memory_space=pltpu.SMEM)
    vmem = pl.BlockSpec(memory_space=pltpu.VMEM)
    hbm = pl.BlockSpec(memory_space=pltpu.HBM)
    anywhere = pl.BlockSpec(memory_space=pl.ANY)
    slots = 9
    turned = pltpu.with_memory_space_constraint(shapes.T, pltpu.HBM)
    owners = pltpu.with_memory_space_constraint(owners, pltpu.HBM)
    new, update, norms = pl.pallas_call(
        functools.partial(kernel, mats, n_dp, n_zero),
        out_shape=(
            jax.ShapeDtypeStruct((mats, shard, short), F32),
            jax.ShapeDtypeStruct((mats, shard, short), BF16),
            jax.ShapeDtypeStruct((8, 128), F32),
        ),
        in_specs=[smem, smem, hbm, hbm],
        out_specs=(anywhere, anywhere, vmem),
        scratch_shapes=[
            pltpu.VMEM((mats, shard, short), BF16),
            pltpu.VMEM((mats, shard, short), F32),
            pltpu.VMEM((mats, shard, short), BF16),
            pltpu.VMEM((mats, shard, short), F32),
            pltpu.VMEM((shard, short), BF16),
            pltpu.VMEM((n_zero, 8, 128), F32),
            pltpu.VMEM((2, slots, shard, short), BF16),
            pltpu.VMEM((2, slots, shard, short), BF16),
            pltpu.VMEM((128, short), BF16),
            pltpu.VMEM((3 * short // 2, short // 2), F32),
            pltpu.VMEM((n_zero, 3 * short // n_zero, short // 2), F32),
            pltpu.VMEM((3 * short // 2, short // 2), F32),
            pltpu.SemaphoreType.DMA((2,)),
            pltpu.SemaphoreType.DMA((2,)),
            pltpu.SemaphoreType.REGULAR((4,)),
            pltpu.SemaphoreType.DMA((len(PARTS), 2, slots)),
            pltpu.SemaphoreType.DMA((len(PARTS), 2, slots)),
            pltpu.SemaphoreType.DMA((2, len(PARTS), 2, slots)),
            pltpu.SemaphoreType.DMA((2, len(PARTS), 2, slots)),
            pltpu.SemaphoreType.DMA((3,)),
            pltpu.SemaphoreType.DMA((3,)),
        ],
        compiler_params=pltpu.CompilerParams(
            collective_id=0, has_side_effects=True, vmem_limit_bytes=24 * 1024 * 1024
        ),
    )(turned, owners, *(pltpu.with_memory_space_constraint(a, pltpu.HBM) for a in (grad_partial, momentum)))
    return pl.pallas_call(
        finish,
        out_shape=(
            jax.ShapeDtypeStruct((mats, shard, short), F32),
            jax.ShapeDtypeStruct((mats, shard, short), BF16),
            jax.ShapeDtypeStruct((1, 1), F32),
        ),
        in_specs=[anywhere, anywhere, vmem],
        out_specs=(anywhere, anywhere, vmem),
        scratch_shapes=[pltpu.SemaphoreType.DMA((2,))],
        compiler_params=pltpu.CompilerParams(vmem_limit_bytes=24 * 1024 * 1024),
    )(new, update, norms)


def solution(mesh):
    in_specs = (P("dp", None, "zero", None), P(None, "zero", None), P(), P())
    out_specs = (P(None, "zero", None), P(None, "zero", None), P("zero", None))
    return jax.shard_map(
        functools.partial(per_device, mesh.shape["dp"], mesh.shape["zero"]),
        mesh=mesh, in_specs=in_specs, out_specs=out_specs, check_vma=False,
    )
```
